32 devices in a mesh: seq: 4 (over y, x), ctx: 8 (over z, core).
Axes of the slice: x: 2, y: 2, z: 4, core: 2. Of those that a mesh axis runs over, the one named last changes fastest.
Arguments:
- tokens: bfloat16 [16, 768, 768], P('seq', 'ctx'), may hold values from -6 to 6
- query_key_value_matrix: bfloat16 [768, 2304], P('seq'), may hold values from -0.21875 to 0.21875
- attention_output_matrix: bfloat16 [768, 768], P('seq'), may hold values from -6 to 6
- gate_up_matrix: bfloat16 [768, 2304], P('seq'), may hold values from -0.21875 to 0.21875
- feedforward_output_matrix: bfloat16 [1152, 768], P('seq'), may hold values from -0.1875 to 0.1875
- gain_attn: bfloat16 [768], P('seq'), may hold values from 0.099609375 to 1.8984375
- gain_mlp: bfloat16 [768], P('seq'), may hold values from 0.099609375 to 1.8984375
- cotangent: bfloat16 [16, 768, 768], P('seq', 'ctx'), may hold values from -6 to 6
Outputs:
- layer_output: bfloat16 [16, 768, 768], P('seq', 'ctx')
- grad_tokens: float32 [16, 768, 768], P('seq', 'ctx')
- grad_w_qkv: float32 [768, 2304], P('seq')
- grad_w_attn_out: float32 [768, 768], P('seq')
- grad_w_in: float32 [768, 2304], P('seq')
- grad_w_mlp_out: float32 [1152, 768], P('seq')
- grad_gain_attn: float32 [768], P('seq')
- grad_gain_mlp: float32 [768], P('seq')
The draws below stay inside these ranges and needn't reach their ends.
All inputs are finite; a program needn't handle non-finite values.
Results may differ from the reference program's by a relative error of at most 0.024.
Values may be sent and summed in bfloat16 or wider, within the bound.
A program may use at most 192 MiB of HBM per device.

```python
import jax
import jax.numpy as jnp
from jax import lax

D = 768
H = 12
HD = 64
FF = 1152
LEN = 768
SEQS = 16


def block_scale(rng, shape, cuts, low, largest):
    loudness, own = 1.0, jax.random.fold_in(rng, 6)
    for position, blocks in cuts:
        heights = jnp.exp(jax.random.uniform(jax.random.fold_in(own, position), (blocks,), jnp.float32, low / len(cuts), largest / len(cuts)))
        loudness = loudness * jnp.repeat(heights, shape[position] // blocks).reshape([-1 if axis == position else 1 for axis in range(len(shape))])
    return loudness


def noise(own_key, extent, spread, limit, cuts=(), kind=jnp.bfloat16):
    drawn = spread * jax.random.normal(own_key, extent, jnp.float32)
    if cuts:
        drawn = drawn * block_scale(own_key, extent, cuts, -0.22, 0.18)
    return jnp.clip(drawn, -limit, limit).astype(kind)


def setup_inputs(seed: int = 0) -> dict:
    keys = jax.random.split(jax.random.key(seed), 9)
    return {
        "tokens": noise(keys[0], (SEQS, LEN, D), 1.0, 6.0, ((0, 4), (1, 8))),
        "query_key_value_matrix": noise(keys[1], (D, 3 * D), D ** -0.5, 0.21875, ((0, 4),)),
        "attention_output_matrix": noise(keys[2], (D, D), 1 ** -0.5, 6.0, ((0, 4),)),
        "gate_up_matrix": noise(keys[3], (D, 2 * FF), D ** -0.5, 0.21875, ((0, 4),)),
        "feedforward_output_matrix": noise(keys[4], (FF, D), FF ** -0.5, 0.1875, ((0, 4),)),
        "gain_attn": jnp.clip(1.0 + 0.18 * jax.random.normal(keys[5], (D,), jnp.float32), 0.099609375, 1.8984375).astype(jnp.bfloat16),
        "gain_mlp": jnp.clip(1.0 + 0.18 * jax.random.normal(keys[6], (D,), jnp.float32), 0.099609375, 1.8984375).astype(jnp.bfloat16),
        "cotangent": noise(keys[7], (SEQS, LEN, D), 1.0, 6.0, ((0, 4), (1, 8))),
    }


rope_base = 160000.0
norm_eps = 1e-05
maximal_precision = lax.Precision.HIGHEST

@jax.custom_vjp
def low(v):
    return lax.optimization_barrier(v.astype(jnp.bfloat16)).astype(jnp.float32)

@jax.custom_vjp
def lowered_backward(v):
    return v

def low_keep(v):
    return (low(v), None)

def low_pass(kept, grad):
    return (grad,)

def back_keep(v):
    return (v, None)

def back_low(kept, grad):
    return (low(grad),)
low.defvjp(low_keep, low_pass)
lowered_backward.defvjp(back_keep, back_low)

def layer_norm(values_in, gain_vector):
    average = lax.optimization_barrier(jnp.mean(values_in, axis=-1, keepdims=True))
    centred = values_in - average
    variance = lax.optimization_barrier(jnp.mean(centred * centred, axis=-1, keepdims=True))
    return centred * lax.rsqrt(variance + norm_eps) * gain_vector

def angle_tables(positions):
    half_size = HD // 2
    frequency = rope_base ** (-(jnp.arange(half_size, dtype=jnp.float32) * 2.0) / HD)
    angles = positions[:, None] * frequency[None, :]
    angles = jnp.concatenate([angles, angles], axis=-1)
    return (jnp.cos(angles), jnp.sin(angles))

def rotate(heads, cosine_table, sine_table):
    half_size = heads.shape[-1] // 2
    front_half = heads[..., :half_size]
    back_half = heads[..., half_size:]
    turned = jnp.concatenate([-back_half, front_half], axis=-1)
    return heads * cosine_table[:, None, :] + turned * sine_table[:, None, :]

def attend_sequence(query_heads, key_heads, value_heads):
    query_block = 512 if LEN % 512 == 0 else LEN
    block_count = LEN // query_block

    def one_block(query_rows):
        scores = lowered_backward(jnp.einsum('qhd,khd->hqk', query_rows, key_heads, precision=maximal_precision) * 0.125)
        log_total = jax.nn.logsumexp(scores, axis=-1, keepdims=True)
        probabilities = low(jnp.exp(scores - log_total))
        return jnp.einsum('hqk,khd->qhd', probabilities, value_heads, precision=maximal_precision)
    attention_result = lax.map(jax.checkpoint(one_block), query_heads.reshape(block_count, query_block, H, HD))
    return attention_result.reshape(LEN, H, HD)

def forward(inputs, query_key_value_matrix, attention_output_matrix, gate_up_matrix, feedforward_output_matrix, gain_attn, gain_mlp):
    first_normalized = low(layer_norm(inputs, gain_attn))
    query_key_value = lowered_backward(jnp.einsum('jka,an->jkn', first_normalized, query_key_value_matrix, precision=maximal_precision))
    cosine_table, sine_table = angle_tables(jnp.arange(LEN, dtype=jnp.float32))
    head_shape = (SEQS, LEN, H, HD)
    query_heads = low(rotate(query_key_value[..., :D].reshape(head_shape), cosine_table, sine_table))
    key_heads = low(rotate(query_key_value[..., D:2 * D].reshape(head_shape), cosine_table, sine_table))
    value_heads = low(query_key_value[..., 2 * D:].reshape(head_shape))
    attention_result = lax.map(lambda triple_heads: attend_sequence(triple_heads[0], triple_heads[1], triple_heads[2]), (query_heads, key_heads, value_heads))
    attention_result = low(lowered_backward(attention_result.reshape(SEQS, LEN, D)))
    residual_branch = lowered_backward(jnp.einsum('jka,an->jkn', attention_result, attention_output_matrix, precision=maximal_precision))
    middle = inputs + residual_branch
    second_normalized = low(layer_norm(middle, gain_mlp))
    gate_up_product = lowered_backward(jnp.einsum('uvc,cw->uvw', second_normalized, gate_up_matrix, precision=maximal_precision))
    mixed_hidden_state = low(jax.nn.gelu(gate_up_product[..., :FF], approximate=False) * gate_up_product[..., FF:])
    feedforward_output = lowered_backward(jnp.einsum('umz,zy->umy', mixed_hidden_state, feedforward_output_matrix, precision=maximal_precision))
    return middle + feedforward_output

def reference(tokens, query_key_value_matrix, attention_output_matrix, gate_up_matrix, feedforward_output_matrix, gain_attn, gain_mlp, cotangent):
    primals = tuple((array_in.astype(jnp.float32) for array_in in (tokens, query_key_value_matrix, attention_output_matrix, gate_up_matrix, feedforward_output_matrix, gain_attn, gain_mlp)))
    output, pullback = jax.vjp(forward, *primals)
    grads = pullback(cotangent.astype(jnp.float32))
    return (output.astype(jnp.bfloat16), grads[0], grads[1], grads[2], grads[3], grads[4], grads[5], grads[6])
```

```python
import functools

import jax
import jax.numpy as jnp
from jax import lax
from jax.experimental import pallas as pl
from jax.experimental.pallas import tpu as pltpu
from jax.sharding import PartitionSpec as P

H = 12
HD = 64
FF = 1152
PAIR = 2 * HD

rope_base = 160000.0
norm_eps = 1e-05
f32 = jnp.float32
bf16 = jnp.bfloat16


def dot(a, b, dims):
    return lax.dot_general(a, b, (dims, ((), ())), preferred_element_type=f32)


NN = ((1,), (0,))
NT = ((1,), (1,))
TN = ((0,), (0,))


def attend_kernel(q_ref, k_ref, v_ref, o_ref, lse_ref):
    outs, totals = [], []
    for half in range(2):
        cols = slice(half * HD, (half + 1) * HD)
        scores = dot(q_ref[:, cols], k_ref[:, cols], NT) * 0.125
        largest = jnp.max(scores, axis=-1, keepdims=True)
        weights = jnp.exp(scores - largest)
        total = jnp.sum(weights, axis=-1, keepdims=True)
        outs.append(dot(weights.astype(bf16), v_ref[:, cols], NN) / total)
        totals.append(jnp.broadcast_to(largest + jnp.log(total), outs[-1].shape))
    o_ref[...] = jnp.concatenate(outs, axis=-1).astype(bf16)
    lse_ref[...] = jnp.concatenate(totals, axis=-1)


def attend_back_kernel(q_ref, k_ref, v_ref, do_ref, lse_ref, dq_ref, dk_ref, dv_ref):
    dqs, dks, dvs = [], [], []
    for half in range(2):
        cols = slice(half * HD, (half + 1) * HD)
        q, k, v, do = q_ref[:, cols], k_ref[:, cols], v_ref[:, cols], do_ref[:, cols]
        scores = dot(q, k, NT) * 0.125
        probabilities = jnp.exp(scores - lse_ref[:, half * HD : half * HD + 1])
        grad_probs = dot(do, v, NT)
        delta = jnp.sum(probabilities * grad_probs, axis=-1, keepdims=True)
        grad_scores = (probabilities * (grad_probs - delta)).astype(bf16)
        dqs.append(dot(grad_scores, k, NN) * 0.125)
        dks.append(dot(grad_scores, q, TN) * 0.125)
        dvs.append(dot(probabilities.astype(bf16), do, TN))
    dq_ref[...] = jnp.concatenate(dqs, axis=-1)
    dk_ref[...] = jnp.concatenate(dks, axis=-1).astype(bf16)
    dv_ref[...] = jnp.concatenate(dvs, axis=-1).astype(bf16)


def column_blocks(rows):
    return pl.BlockSpec((rows, PAIR), lambda h: (0, h))


def attend(q, k, v):
    rows, width = q.shape
    keys = k.shape[0]
    return pl.pallas_call(
        attend_kernel,
        grid=(width // PAIR,),
        in_specs=[column_blocks(rows), column_blocks(keys), column_blocks(keys)],
        out_specs=[column_blocks(rows), column_blocks(rows)],
        out_shape=[
            jax.ShapeDtypeStruct((rows, width), bf16),
            jax.ShapeDtypeStruct((rows, width), f32),
        ],
        compiler_params=pltpu.CompilerParams(vmem_limit_bytes=50 * 2**20),
        cost_estimate=pl.CostEstimate(
            flops=4 * rows * keys * width,
            bytes_accessed=8 * (rows + keys) * width,
            transcendentals=rows * keys * H,
        ),
    )(q, k, v)


def attend_back(q, k, v, do, lse):
    rows, width = q.shape
    keys = k.shape[0]
    return pl.pallas_call(
        attend_back_kernel,
        grid=(width // PAIR,),
        in_specs=[
            column_blocks(rows),
            column_blocks(keys),
            column_blocks(keys),
            column_blocks(rows),
            column_blocks(rows),
        ],
        out_specs=[column_blocks(rows), column_blocks(keys), column_blocks(keys)],
        out_shape=[
            jax.ShapeDtypeStruct((rows, width), f32),
            jax.ShapeDtypeStruct((keys, width), bf16),
            jax.ShapeDtypeStruct((keys, width), bf16),
        ],
        compiler_params=pltpu.CompilerParams(vmem_limit_bytes=50 * 2**20),
        cost_estimate=pl.CostEstimate(
            flops=10 * rows * keys * width,
            bytes_accessed=12 * (rows + keys) * width,
            transcendentals=rows * keys * H,
        ),
    )(q, k, v, do, lse)


def turn(values):
    column = lax.broadcasted_iota(jnp.int32, values.shape, 1)
    ahead = jnp.concatenate([values[:, HD // 2 :], values[:, : HD // 2]], axis=1)
    behind = jnp.concatenate([values[:, -(HD // 2) :], values[:, : -(HD // 2)]], axis=1)
    return jnp.where(column % HD < HD // 2, -ahead, behind)


def rotate(values, cosines, sines):
    return values * cosines + turn(values) * sines


def unrotate(values, cosines, sines):
    return values * cosines - turn(values * sines)


def normalize(values):
    average = jnp.mean(values, axis=-1, keepdims=True)
    centred = values - average
    variance = jnp.mean(centred * centred, axis=-1, keepdims=True)
    scale = lax.rsqrt(variance + norm_eps)
    return centred * scale, scale


def norm_back(e, xhat, scale):
    return scale * (
        e - jnp.mean(e, axis=-1, keepdims=True) - xhat * jnp.mean(e * xhat, axis=-1, keepdims=True)
    )


def body(seqs_here, group, tokens, w_qkv, w_attn, w_in, w_mlp, gain_one, gain_two, cotangent):
    block_rows, width = tokens.shape[1:]
    ctx = seqs_here * group
    me = lax.axis_index("ctx")
    mine, place = me // group, me % group

    def hop(block, distance):
        route = [(i, (i + distance * group) % ctx) for i in range(ctx)]
        return lax.ppermute(block, "ctx", route)

    def to_sequence(values):
        parts = [lax.dynamic_index_in_dim(values, mine, 0, keepdims=False)]
        for d in range(1, seqs_here):
            part = lax.dynamic_index_in_dim(values, (mine + d) % seqs_here, 0, keepdims=False)
            parts.append(hop(part, d))
        return jnp.concatenate(parts, axis=0)

    def from_sequence(values):
        parts = [values[:block_rows]]
        for d in range(1, seqs_here):
            parts.append(hop(values[d * block_rows : (d + 1) * block_rows], -d))
        stacked = jnp.stack(parts + parts)
        return lax.dynamic_slice_in_dim(stacked, (seqs_here - mine) % seqs_here, seqs_here, 0)

    groups = [[q * group + r for r in range(group)] for q in range(seqs_here)]
    swap = [(i, i ^ 1) for i in range(ctx)]

    def share_keys(k, v):
        if group == 2:
            other = lax.ppermute(jnp.stack([k, v]), "ctx", swap)
            return jnp.concatenate([k, other[0]]), jnp.concatenate([v, other[1]])
        both = lax.all_gather(jnp.stack([k, v]), "ctx", axis=1, tiled=True, axis_index_groups=groups)
        return both[0], both[1]

    def sum_keys(dk, dv):
        rows = dk.shape[0] // group
        if group == 2:
            other = lax.ppermute(jnp.stack([dk[rows:], dv[rows:]]), "ctx", swap)
            return (
                dk[:rows].astype(f32) + other[0].astype(f32),
                dv[:rows].astype(f32) + other[1].astype(f32),
            )
        both = lax.psum_scatter(
            jnp.stack([dk, dv]), "ctx", scatter_dimension=1, axis_index_groups=groups, tiled=True
        ).astype(f32)
        return both[0], both[1]

    def gather(shard):
        return lax.all_gather(shard, "seq", axis=0, tiled=True)

    def reduce_shard(grad):
        part = lax.psum_scatter(grad.astype(bf16), "seq", scatter_dimension=0, tiled=True)
        return lax.psum(part, "ctx").astype(f32)

    gain_one = gain_one.astype(f32)[:, None]
    gain_two = gain_two.astype(f32)[:, None]
    qkv_all = gather((w_qkv.astype(f32) * gain_one).astype(bf16))
    attn_all = gather(w_attn)
    in_all = gather((w_in.astype(f32) * gain_two).astype(bf16))
    mlp_all = gather(w_mlp)

    x = to_sequence(tokens).astype(f32)
    g = to_sequence(cotangent)

    came_from = (mine - jnp.arange(seqs_here, dtype=jnp.int32)) % seqs_here
    starts = (came_from * group + place) * block_rows
    positions = (starts[:, None] + jnp.arange(block_rows, dtype=jnp.int32)).reshape(-1)
    frequency = rope_base ** (-(jnp.arange(HD // 2, dtype=f32) * 2.0) / HD)
    angles = positions.astype(f32)[:, None] * frequency[None, :]
    cosines = jnp.tile(jnp.cos(angles), (1, 2 * H))
    sines = jnp.tile(jnp.sin(angles), (1, 2 * H))

    xhat, scale_one = normalize(x)
    h1 = xhat.astype(bf16)
    qkv = dot(h1, qkv_all, NN)
    q = rotate(qkv[:, :width], cosines, sines).astype(bf16)
    k = rotate(qkv[:, width : 2 * width], cosines, sines).astype(bf16)
    v = qkv[:, 2 * width :].astype(bf16)
    keys, values = share_keys(k, v)
    attn, lse = attend(q, keys, values)
    x2 = x + dot(attn, attn_all, NN)
    xhat2, scale_two = normalize(x2)
    h2 = xhat2.astype(bf16)
    gu = dot(h2, in_all, NN)
    gate, up = gu[:, :FF], gu[:, FF:]
    cumulative = 0.5 * (1.0 + lax.erf(gate * (0.5**0.5)))
    gelu = gate * cumulative
    slope = cumulative + gate * jnp.exp(-0.5 * gate * gate) * 0.3989422804014327
    a = (gelu * up).astype(bf16)
    layer_output = from_sequence((x2 + dot(a, mlp_all, NN)).astype(bf16))
    grad_mlp = reduce_shard(dot(a, g, TN))
    da = dot(g, mlp_all, NT)
    dgu = jnp.concatenate([da * up * slope, da * gelu], axis=-1).astype(bf16)
    raw_in = reduce_shard(dot(h2, dgu, TN))
    dx2 = g.astype(f32) + norm_back(dot(dgu, in_all, NT), xhat2, scale_two)
    dy = dx2.astype(bf16)
    grad_attn = reduce_shard(dot(attn, dy, TN))
    do = dot(dy, attn_all, NT).astype(bf16)
    dq, dk, dv = attend_back(q, keys, values, do, lse)
    dk, dv = sum_keys(dk, dv)
    dqkv = jnp.concatenate(
        [unrotate(dq, cosines, sines), unrotate(dk, cosines, sines), dv], axis=-1
    ).astype(bf16)
    raw_qkv = reduce_shard(dot(h1, dqkv, TN))
    dx = dx2 + norm_back(dot(dqkv, qkv_all, NT), xhat, scale_one)
    grad_tokens = from_sequence(dx.astype(bf16)).astype(f32)
    return (
        layer_output,
        grad_tokens,
        raw_qkv * gain_one,
        grad_attn,
        raw_in * gain_two,
        grad_mlp,
        jnp.sum(raw_qkv * w_qkv.astype(f32), axis=-1),
        jnp.sum(raw_in * w_in.astype(f32), axis=-1),
    )


def solution(mesh):
    split = P("seq", "ctx", None)
    rows = P("seq", None)

    def whole(tokens, *others):
        seqs_here = tokens.shape[0] // mesh.shape["seq"]
        group = mesh.shape["ctx"] // seqs_here
        return jax.shard_map(
            functools.partial(body, seqs_here, group),
            mesh=mesh,
            in_specs=(split, rows, rows, rows, rows, P("seq"), P("seq"), split),
            out_specs=(split, split, rows, rows, rows, rows, P("seq"), P("seq")),
            check_vma=False,
        )(tokens, *others)

    return whole
```

```python
import functools

import jax
import jax.numpy as jnp
from jax import lax
from jax.experimental import pallas as pl
from jax.experimental.pallas import tpu as pltpu
from jax.sharding import PartitionSpec as P

H = 12
HD = 64
FF = 1152
PAIR = 2 * HD

rope_base = 160000.0
norm_eps = 1e-05
f32 = jnp.float32
bf16 = jnp.bfloat16


def dot(a, b, dims):
    return lax.dot_general(a, b, (dims, ((), ())), preferred_element_type=f32)


NN = ((1,), (0,))
NT = ((1,), (1,))
TN = ((0,), (0,))


def attend_kernel(q_ref, k_ref, v_ref, o_ref, lse_ref):
    outs, totals = [], []
    for half in range(2):
        cols = slice(half * HD, (half + 1) * HD)
        scores = dot(q_ref[:, cols], k_ref[:, cols], NT) * 0.125
        largest = jnp.max(scores, axis=-1, keepdims=True)
        weights = jnp.exp(scores - largest)
        total = jnp.sum(weights, axis=-1, keepdims=True)
        outs.append(dot(weights.astype(bf16), v_ref[:, cols], NN) / total)
        totals.append(jnp.broadcast_to(largest + jnp.log(total), outs[-1].shape))
    o_ref[...] = jnp.concatenate(outs, axis=-1).astype(bf16)
    lse_ref[...] = jnp.concatenate(totals, axis=-1)


def attend_back_kernel(q_ref, k_ref, v_ref, do_ref, lse_ref, dq_ref, dk_ref, dv_ref):
    dqs, dks, dvs = [], [], []
    for half in range(2):
        cols = slice(half * HD, (half + 1) * HD)
        q, k, v, do = q_ref[:, cols], k_ref[:, cols], v_ref[:, cols], do_ref[:, cols]
        scores = dot(q, k, NT) * 0.125
        probabilities = jnp.exp(scores - lse_ref[:, half * HD : half * HD + 1])
        grad_probs = dot(do, v, NT)
        delta = jnp.sum(probabilities * grad_probs, axis=-1, keepdims=True)
        grad_scores = (probabilities * (grad_probs - delta)).astype(bf16)
        dqs.append(dot(grad_scores, k, NN) * 0.125)
        dks.append(dot(grad_scores, q, TN) * 0.125)
        dvs.append(dot(probabilities.astype(bf16), do, TN))
    dq_ref[...] = jnp.concatenate(dqs, axis=-1)
    dk_ref[...] = jnp.concatenate(dks, axis=-1).astype(bf16)
    dv_ref[...] = jnp.concatenate(dvs, axis=-1).astype(bf16)


def column_blocks(rows):
    return pl.BlockSpec((rows, PAIR), lambda h: (0, h))


def attend(q, k, v):
    rows, width = q.shape
    keys = k.shape[0]
    return pl.pallas_call(
        attend_kernel,
        grid=(width // PAIR,),
        in_specs=[column_blocks(rows), column_blocks(keys), column_blocks(keys)],
        out_specs=[column_blocks(rows), column_blocks(rows)],
        out_shape=[
            jax.ShapeDtypeStruct((rows, width), bf16),
            jax.ShapeDtypeStruct((rows, width), f32),
        ],
        compiler_params=pltpu.CompilerParams(vmem_limit_bytes=50 * 2**20),
        cost_estimate=pl.CostEstimate(
            flops=4 * rows * keys * width,
            bytes_accessed=8 * (rows + keys) * width,
            transcendentals=rows * keys * H,
        ),
    )(q, k, v)


def attend_back(q, k, v, do, lse):
    rows, width = q.shape
    keys = k.shape[0]
    return pl.pallas_call(
        attend_back_kernel,
        grid=(width // PAIR,),
        in_specs=[
            column_blocks(rows),
            column_blocks(keys),
            column_blocks(keys),
            column_blocks(rows),
            column_blocks(rows),
        ],
        out_specs=[column_blocks(rows), column_blocks(keys), column_blocks(keys)],
        out_shape=[
            jax.ShapeDtypeStruct((rows, width), f32),
            jax.ShapeDtypeStruct((keys, width), bf16),
            jax.ShapeDtypeStruct((keys, width), bf16),
        ],
        compiler_params=pltpu.CompilerParams(vmem_limit_bytes=50 * 2**20),
        cost_estimate=pl.CostEstimate(
            flops=10 * rows * keys * width,
            bytes_accessed=12 * (rows + keys) * width,
            transcendentals=rows * keys * H,
        ),
    )(q, k, v, do, lse)


def turn(values):
    column = lax.broadcasted_iota(jnp.int32, values.shape, 1)
    ahead = jnp.concatenate([values[:, HD // 2 :], values[:, : HD // 2]], axis=1)
    behind = jnp.concatenate([values[:, -(HD // 2) :], values[:, : -(HD // 2)]], axis=1)
    return jnp.where(column % HD < HD // 2, -ahead, behind)


def rotate(values, cosines, sines):
    return values * cosines + turn(values) * sines


def unrotate(values, cosines, sines):
    return values * cosines - turn(values * sines)


def normalize(values):
    average = jnp.mean(values, axis=-1, keepdims=True)
    centred = values - average
    variance = jnp.mean(centred * centred, axis=-1, keepdims=True)
    scale = lax.rsqrt(variance + norm_eps)
    return centred * scale, scale


def norm_back(e, xhat, scale):
    return scale * (
        e - jnp.mean(e, axis=-1, keepdims=True) - xhat * jnp.mean(e * xhat, axis=-1, keepdims=True)
    )


def body(seqs_here, group, tokens, w_qkv, w_attn, w_in, w_mlp, gain_one, gain_two, cotangent):
    block_rows, width = tokens.shape[1:]
    ctx = seqs_here * group
    me = lax.axis_index("ctx")
    mine, place = me // group, me % group

    def hop(block, distance):
        route = [(i, (i + distance * group) % ctx) for i in range(ctx)]
        return lax.ppermute(block, "ctx", route)

    def to_sequence(values):
        parts = [lax.dynamic_index_in_dim(values, mine, 0, keepdims=False)]
        for d in range(1, seqs_here):
            part = lax.dynamic_index_in_dim(values, (mine + d) % seqs_here, 0, keepdims=False)
            parts.append(hop(part, d))
        return jnp.concatenate(parts, axis=0)

    def from_sequence(values):
        parts = [values[:block_rows]]
        for d in range(1, seqs_here):
            parts.append(hop(values[d * block_rows : (d + 1) * block_rows], -d))
        stacked = jnp.stack(parts + parts)
        return lax.dynamic_slice_in_dim(stacked, (seqs_here - mine) % seqs_here, seqs_here, 0)

    groups = [[q * group + r for r in range(group)] for q in range(seqs_here)]
    swap = [(i, i ^ 1) for i in range(ctx)]

    def share_keys(k, v):
        if group == 2:
            other = lax.ppermute(jnp.stack([k, v]), "ctx", swap)
            return jnp.concatenate([k, other[0]]), jnp.concatenate([v, other[1]])
        both = lax.all_gather(jnp.stack([k, v]), "ctx", axis=1, tiled=True, axis_index_groups=groups)
        return both[0], both[1]

    def sum_keys(dk, dv):
        rows = dk.shape[0] // group
        if group == 2:
            other = lax.ppermute(jnp.stack([dk[rows:], dv[rows:]]), "ctx", swap)
            return (
                dk[:rows].astype(f32) + other[0].astype(f32),
                dv[:rows].astype(f32) + other[1].astype(f32),
            )
        both = lax.psum_scatter(
            jnp.stack([dk, dv]), "ctx", scatter_dimension=1, axis_index_groups=groups, tiled=True
        ).astype(f32)
        return both[0], both[1]

    core = me % 2
    parity = [[i for i in range(ctx) if i % 2 == r] for r in range(2)]

    def half_of(values, which):
        half = values.shape[1] // 2
        return lax.dynamic_slice_in_dim(values, which * half, half, 1)

    def join(own, other):
        left = jnp.where(core == 0, own, other)
        right = jnp.where(core == 0, other, own)
        return jnp.concatenate([left, right], axis=1)

    def gather(shard):
        return lax.all_gather(half_of(shard, core), "seq", axis=0, tiled=True)

    def both_halves(own):
        return join(own, lax.ppermute(own, "ctx", swap))

    def reduce_pair(left, right):
        sent = dot(left, half_of(right, 1 - core), TN).astype(bf16)
        got = lax.ppermute(sent, "ctx", swap)
        kept = dot(left, half_of(right, core), TN) + got.astype(f32)
        return kept.astype(bf16)

    def scatter(kept):
        return lax.psum_scatter(kept, "seq", scatter_dimension=0, tiled=True)

    def reduce_ctx(parts):
        totals = lax.psum(parts, "ctx", axis_index_groups=parity)
        return [join(t, lax.ppermute(t, "ctx", swap)).astype(f32) for t in totals]

    gain_one = gain_one.astype(f32)[:, None]
    gain_two = gain_two.astype(f32)[:, None]
    qkv_all = both_halves(gather((w_qkv.astype(f32) * gain_one).astype(bf16)))
    attn_all = gather(w_attn)
    in_all = gather((w_in.astype(f32) * gain_two).astype(bf16))
    mlp_all = gather(w_mlp)

    x = to_sequence(tokens).astype(f32)
    g = to_sequence(cotangent)

    came_from = (mine - jnp.arange(seqs_here, dtype=jnp.int32)) % seqs_here
    starts = (came_from * group + place) * block_rows
    positions = (starts[:, None] + jnp.arange(block_rows, dtype=jnp.int32)).reshape(-1)
    frequency = rope_base ** (-(jnp.arange(HD // 2, dtype=f32) * 2.0) / HD)
    angles = positions.astype(f32)[:, None] * frequency[None, :]
    cosines = jnp.tile(jnp.cos(angles), (1, 2 * H))
    sines = jnp.tile(jnp.sin(angles), (1, 2 * H))

    xhat, scale_one = normalize(x)
    h1 = xhat.astype(bf16)
    qkv = dot(h1, qkv_all, NN)
    q = rotate(qkv[:, :width], cosines, sines).astype(bf16)
    k = rotate(qkv[:, width : 2 * width], cosines, sines).astype(bf16)
    v = qkv[:, 2 * width :].astype(bf16)
    keys, values = share_keys(k, v)
    attn_all = both_halves(attn_all)
    attn, lse = attend(q, keys, values)
    attn, in_all, mlp_all = lax.optimization_barrier((attn, in_all, mlp_all))
    in_all, mlp_all = both_halves(in_all), both_halves(mlp_all)
    x2 = x + dot(attn, attn_all, NN)
    xhat2, scale_two = normalize(x2)
    h2 = xhat2.astype(bf16)
    gu = dot(h2, in_all, NN)
    gate, up = gu[:, :FF], gu[:, FF:]
    cumulative = 0.5 * (1.0 + lax.erf(gate * (0.5**0.5)))
    gelu = gate * cumulative
    slope = cumulative + gate * jnp.exp(-0.5 * gate * gate) * 0.3989422804014327
    a = (gelu * up).astype(bf16)
    layer_output = from_sequence((x2 + dot(a, mlp_all, NN)).astype(bf16))
    part_mlp = reduce_pair(a, g)
    da = dot(g, mlp_all, NT)
    dgu = jnp.concatenate([da * up * slope, da * gelu], axis=-1).astype(bf16)
    part_in = reduce_pair(h2, dgu)
    dx2 = g.astype(f32) + norm_back(dot(dgu, in_all, NT), xhat2, scale_two)
    dy = dx2.astype(bf16)
    part_attn = reduce_pair(attn, dy)
    do = dot(dy, attn_all, NT).astype(bf16)
    do, part_mlp, part_in, part_attn = lax.optimization_barrier((do, part_mlp, part_in, part_attn))
    parts = [scatter(part_mlp), scatter(part_in), scatter(part_attn)]
    grad_mlp, raw_in, grad_attn = reduce_ctx(parts)
    dq, dk, dv = attend_back(q, keys, values, do, lse)
    dk, dv = sum_keys(dk, dv)
    dqkv = jnp.concatenate(
        [unrotate(dq, cosines, sines), unrotate(dk, cosines, sines), dv], axis=-1
    ).astype(bf16)
    part_qkv = scatter(reduce_pair(h1, dqkv))
    part_qkv, grad_mlp, raw_in, grad_attn = lax.optimization_barrier(
        (part_qkv, grad_mlp, raw_in, grad_attn)
    )
    (raw_qkv,) = reduce_ctx([part_qkv])
    dx = dx2 + norm_back(dot(dqkv, qkv_all, NT), xhat, scale_one)
    grad_tokens = from_sequence(dx.astype(bf16)).astype(f32)
    return (
        layer_output,
        grad_tokens,
        raw_qkv * gain_one,
        grad_attn,
        raw_in * gain_two,
        grad_mlp,
        jnp.sum(raw_qkv * w_qkv.astype(f32), axis=-1),
        jnp.sum(raw_in * w_in.astype(f32), axis=-1),
    )


def solution(mesh):
    split = P("seq", "ctx", None)
    rows = P("seq", None)

    def whole(tokens, *others):
        seqs_here = tokens.shape[0] // mesh.shape["seq"]
        group = mesh.shape["ctx"] // seqs_here
        return jax.shard_map(
            functools.partial(body, seqs_here, group),
            mesh=mesh,
            in_specs=(split, rows, rows, rows, rows, P("seq"), P("seq"), split),
            out_specs=(split, split, rows, rows, rows, rows, P("seq"), P("seq")),
            check_vma=False,
        )(tokens, *others)

    return whole
```

```python
import functools

import jax
import jax.numpy as jnp
from jax import lax
from jax.experimental import pallas as pl
from jax.experimental.pallas import tpu as pltpu
from jax.sharding import PartitionSpec as P

H = 12
HD = 64
FF = 1152
PAIR = 2 * HD

rope_base = 160000.0
norm_eps = 1e-05
f32 = jnp.float32
bf16 = jnp.bfloat16


def dot(a, b, dims):
    return lax.dot_general(a, b, (dims, ((), ())), preferred_element_type=f32)


NN = ((1,), (0,))
NT = ((1,), (1,))
TN = ((0,), (0,))


def attend_kernel(q_ref, k_ref, v_ref, o_ref, lse_ref):
    outs, totals = [], []
    for half in range(2):
        cols = slice(half * HD, (half + 1) * HD)
        scores = dot(q_ref[:, cols], k_ref[:, cols], NT) * 0.125
        largest = jnp.max(scores, axis=-1, keepdims=True)
        weights = jnp.exp(scores - largest)
        total = jnp.sum(weights, axis=-1, keepdims=True)
        outs.append(dot(weights.astype(bf16), v_ref[:, cols], NN) / total)
        totals.append(jnp.broadcast_to(largest + jnp.log(total), outs[-1].shape))
    o_ref[...] = jnp.concatenate(outs, axis=-1).astype(bf16)
    lse_ref[...] = jnp.concatenate(totals, axis=-1)


def attend_back_kernel(q_ref, k_ref, v_ref, do_ref, lse_ref, dq_ref, dk_ref, dv_ref):
    dqs, dks, dvs = [], [], []
    for half in range(2):
        cols = slice(half * HD, (half + 1) * HD)
        q, k, v, do = q_ref[:, cols], k_ref[:, cols], v_ref[:, cols], do_ref[:, cols]
        scores = dot(q, k, NT) * 0.125
        probabilities = jnp.exp(scores - lse_ref[:, half * HD : half * HD + 1])
        grad_probs = dot(do, v, NT)
        delta = jnp.sum(probabilities * grad_probs, axis=-1, keepdims=True)
        grad_scores = (probabilities * (grad_probs - delta)).astype(bf16)
        dqs.append(dot(grad_scores, k, NN) * 0.125)
        dks.append(dot(grad_scores, q, TN) * 0.125)
        dvs.append(dot(probabilities.astype(bf16), do, TN))
    dq_ref[...] = jnp.concatenate(dqs, axis=-1)
    dk_ref[...] = jnp.concatenate(dks, axis=-1).astype(bf16)
    dv_ref[...] = jnp.concatenate(dvs, axis=-1).astype(bf16)


def column_blocks(rows):
    return pl.BlockSpec((rows, PAIR), lambda h: (0, h))


def attend(q, k, v):
    rows, width = q.shape
    keys = k.shape[0]
    return pl.pallas_call(
        attend_kernel,
        grid=(width // PAIR,),
        in_specs=[column_blocks(rows), column_blocks(keys), column_blocks(keys)],
        out_specs=[column_blocks(rows), column_blocks(rows)],
        out_shape=[
            jax.ShapeDtypeStruct((rows, width), bf16),
            jax.ShapeDtypeStruct((rows, width), f32),
        ],
        compiler_params=pltpu.CompilerParams(vmem_limit_bytes=50 * 2**20),
        cost_estimate=pl.CostEstimate(
            flops=4 * rows * keys * width,
            bytes_accessed=8 * (rows + keys) * width,
            transcendentals=rows * keys * H,
        ),
    )(q, k, v)


def attend_back(q, k, v, do, lse):
    rows, width = q.shape
    keys = k.shape[0]
    return pl.pallas_call(
        attend_back_kernel,
        grid=(width // PAIR,),
        in_specs=[
            column_blocks(rows),
            column_blocks(keys),
            column_blocks(keys),
            column_blocks(rows),
            column_blocks(rows),
        ],
        out_specs=[column_blocks(rows), column_blocks(keys), column_blocks(keys)],
        out_shape=[
            jax.ShapeDtypeStruct((rows, width), f32),
            jax.ShapeDtypeStruct((keys, width), bf16),
            jax.ShapeDtypeStruct((keys, width), bf16),
        ],
        compiler_params=pltpu.CompilerParams(vmem_limit_bytes=50 * 2**20),
        cost_estimate=pl.CostEstimate(
            flops=10 * rows * keys * width,
            bytes_accessed=12 * (rows + keys) * width,
            transcendentals=rows * keys * H,
        ),
    )(q, k, v, do, lse)


def turn(values):
    column = lax.broadcasted_iota(jnp.int32, values.shape, 1)
    ahead = jnp.concatenate([values[:, HD // 2 :], values[:, : HD // 2]], axis=1)
    behind = jnp.concatenate([values[:, -(HD // 2) :], values[:, : -(HD // 2)]], axis=1)
    return jnp.where(column % HD < HD // 2, -ahead, behind)


def rotate(values, cosines, sines):
    return values * cosines + turn(values) * sines


def unrotate(values, cosines, sines):
    return values * cosines - turn(values * sines)


def normalize(values):
    average = jnp.mean(values, axis=-1, keepdims=True)
    centred = values - average
    variance = jnp.mean(centred * centred, axis=-1, keepdims=True)
    scale = lax.rsqrt(variance + norm_eps)
    return centred * scale, scale


def norm_back(e, xhat, scale):
    return scale * (
        e - jnp.mean(e, axis=-1, keepdims=True) - xhat * jnp.mean(e * xhat, axis=-1, keepdims=True)
    )


def body(seqs_here, group, tokens, w_qkv, w_attn, w_in, w_mlp, gain_one, gain_two, cotangent):
    block_rows, width = tokens.shape[1:]
    ctx = seqs_here * group
    me = lax.axis_index("ctx")
    mine, place = me // group, me % group

    def hop(block, distance):
        route = [(i, (i + distance * group) % ctx) for i in range(ctx)]
        return lax.ppermute(block, "ctx", route)

    def to_sequence(values):
        parts = [lax.dynamic_index_in_dim(values, mine, 0, keepdims=False)]
        for d in range(1, seqs_here):
            part = lax.dynamic_index_in_dim(values, (mine + d) % seqs_here, 0, keepdims=False)
            parts.append(hop(part, d))
        return jnp.concatenate(parts, axis=0)

    def from_sequence(values):
        parts = [values[:block_rows]]
        for d in range(1, seqs_here):
            parts.append(hop(values[d * block_rows : (d + 1) * block_rows], -d))
        stacked = jnp.stack(parts + parts)
        return lax.dynamic_slice_in_dim(stacked, (seqs_here - mine) % seqs_here, seqs_here, 0)

    groups = [[q * group + r for r in range(group)] for q in range(seqs_here)]
    swap = [(i, i ^ 1) for i in range(ctx)]

    def share_keys(k, v):
        if group == 2:
            other = lax.ppermute(jnp.stack([k, v]), "ctx", swap)
            return jnp.concatenate([k, other[0]]), jnp.concatenate([v, other[1]])
        both = lax.all_gather(jnp.stack([k, v]), "ctx", axis=1, tiled=True, axis_index_groups=groups)
        return both[0], both[1]

    def sum_keys(dk, dv):
        rows = dk.shape[0] // group
        if group == 2:
            other = lax.ppermute(jnp.stack([dk[rows:], dv[rows:]]), "ctx", swap)
            return (
                dk[:rows].astype(f32) + other[0].astype(f32),
                dv[:rows].astype(f32) + other[1].astype(f32),
            )
        both = lax.psum_scatter(
            jnp.stack([dk, dv]), "ctx", scatter_dimension=1, axis_index_groups=groups, tiled=True
        ).astype(f32)
        return both[0], both[1]

    core = me % 2
    parity = [[i for i in range(ctx) if i % 2 == r] for r in range(2)]

    def half_of(values, which):
        half = values.shape[1] // 2
        return lax.dynamic_slice_in_dim(values, which * half, half, 1)

    def join(own, other):
        left = jnp.where(core == 0, own, other)
        right = jnp.where(core == 0, other, own)
        return jnp.concatenate([left, right], axis=1)

    def gather(shard):
        return lax.all_gather(half_of(shard, core), "seq", axis=0, tiled=True)

    def both_halves(own):
        return join(own, lax.ppermute(own, "ctx", swap))

    def reduce_pair(left, right):
        sent = dot(left, half_of(right, 1 - core), TN).astype(bf16)
        got = lax.ppermute(sent, "ctx", swap)
        kept = dot(left, half_of(right, core), TN) + got.astype(f32)
        return kept.astype(bf16)

    def scatter(kept):
        return lax.psum_scatter(kept, "seq", scatter_dimension=0, tiled=True)

    mlp_rows, attn_rows = w_mlp.shape[0], w_attn.shape[0]
    narrow = width // 2

    def pack(mlp, attn, wide):
        wide = wide.reshape(-1, attn_rows, wide.shape[1])
        blocks = [wide[:, :, i : i + narrow] for i in range(0, wide.shape[2], narrow)]
        rows = [mlp.reshape(-1, mlp_rows, narrow), attn.reshape(-1, attn_rows, narrow)]
        return jnp.concatenate(rows + blocks, axis=1)

    def unpack(packed):
        start = mlp_rows + attn_rows
        ends = range(start, packed.shape[1], attn_rows)
        blocks = [packed[:, i : i + attn_rows].reshape(-1, narrow) for i in ends]
        return (
            packed[:, :mlp_rows].reshape(-1, narrow),
            packed[:, mlp_rows:start].reshape(-1, narrow),
            jnp.concatenate(blocks, axis=1),
        )

    def join_packed(own):
        other = lax.ppermute(own, "ctx", swap)
        return [join(a, b) for a, b in zip(unpack(own), unpack(other))]

    gain_one = gain_one.astype(f32)[:, None]
    gain_two = gain_two.astype(f32)[:, None]
    qkv_all = both_halves(gather((w_qkv.astype(f32) * gain_one).astype(bf16)))
    scaled_in = (w_in.astype(f32) * gain_two).astype(bf16)
    packed = pack(half_of(w_mlp, core), half_of(w_attn, core), half_of(scaled_in, core))
    packed = lax.all_gather(packed, "seq", axis=0, tiled=True)

    x = to_sequence(tokens).astype(f32)
    g = to_sequence(cotangent)

    came_from = (mine - jnp.arange(seqs_here, dtype=jnp.int32)) % seqs_here
    starts = (came_from * group + place) * block_rows
    positions = (starts[:, None] + jnp.arange(block_rows, dtype=jnp.int32)).reshape(-1)
    frequency = rope_base ** (-(jnp.arange(HD // 2, dtype=f32) * 2.0) / HD)
    angles = positions.astype(f32)[:, None] * frequency[None, :]
    cosines = jnp.tile(jnp.cos(angles), (1, 2 * H))
    sines = jnp.tile(jnp.sin(angles), (1, 2 * H))

    xhat, scale_one = normalize(x)
    h1 = xhat.astype(bf16)
    qkv = dot(h1, qkv_all, NN)
    q = rotate(qkv[:, :width], cosines, sines).astype(bf16)
    k = rotate(qkv[:, width : 2 * width], cosines, sines).astype(bf16)
    v = qkv[:, 2 * width :].astype(bf16)
    keys, values = share_keys(k, v)
    attn, lse = attend(q, keys, values)
    attn, packed = lax.optimization_barrier((attn, packed))
    mlp_all, attn_all, in_all = join_packed(packed)
    x2 = x + dot(attn, attn_all, NN)
    xhat2, scale_two = normalize(x2)
    h2 = xhat2.astype(bf16)
    gu = dot(h2, in_all, NN)
    gate, up = gu[:, :FF], gu[:, FF:]
    cumulative = 0.5 * (1.0 + lax.erf(gate * (0.5**0.5)))
    gelu = gate * cumulative
    slope = cumulative + gate * jnp.exp(-0.5 * gate * gate) * 0.3989422804014327
    a = (gelu * up).astype(bf16)
    layer_output = from_sequence((x2 + dot(a, mlp_all, NN)).astype(bf16))
    part_mlp = reduce_pair(a, g)
    da = dot(g, mlp_all, NT)
    dgu = jnp.concatenate([da * up * slope, da * gelu], axis=-1).astype(bf16)
    part_in = reduce_pair(h2, dgu)
    dx2 = g.astype(f32) + norm_back(dot(dgu, in_all, NT), xhat2, scale_two)
    dy = dx2.astype(bf16)
    part_attn = reduce_pair(attn, dy)
    do = dot(dy, attn_all, NT).astype(bf16)
    part = pack(part_mlp, part_attn, part_in)
    do, part = lax.optimization_barrier((do, part))
    part = lax.psum(scatter(part), "ctx", axis_index_groups=parity)
    dq, dk, dv = attend_back(q, keys, values, do, lse)
    dk, dv = sum_keys(dk, dv)
    dqkv = jnp.concatenate(
        [unrotate(dq, cosines, sines), unrotate(dk, cosines, sines), dv], axis=-1
    ).astype(bf16)
    part_qkv = scatter(reduce_pair(h1, dqkv))
    part_qkv, part = lax.optimization_barrier((part_qkv, part))
    raw_qkv = both_halves(lax.psum(part_qkv, "ctx", axis_index_groups=parity)).astype(f32)
    grad_mlp, grad_attn, raw_in = [t.astype(f32) for t in join_packed(part)]
    dx = dx2 + norm_back(dot(dqkv, qkv_all, NT), xhat, scale_one)
    grad_tokens = from_sequence(dx.astype(bf16)).astype(f32)
    return (
        layer_output,
        grad_tokens,
        raw_qkv * gain_one,
        grad_attn,
        raw_in * gain_two,
        grad_mlp,
        jnp.sum(raw_qkv * w_qkv.astype(f32), axis=-1),
        jnp.sum(raw_in * w_in.astype(f32), axis=-1),
    )


def solution(mesh):
    split = P("seq", "ctx", None)
    rows = P("seq", None)

    def whole(tokens, *others):
        seqs_here = tokens.shape[0] // mesh.shape["seq"]
        group = mesh.shape["ctx"] // seqs_here
        return jax.shard_map(
            functools.partial(body, seqs_here, group),
            mesh=mesh,
            in_specs=(split, rows, rows, rows, rows, P("seq"), P("seq"), split),
            out_specs=(split, split, rows, rows, rows, rows, P("seq"), P("seq")),
            check_vma=False,
        )(tokens, *others)

    return whole
```

```python
import functools

import jax
import jax.numpy as jnp
from jax import lax
from jax.experimental import pallas as pl
from jax.experimental.pallas import tpu as pltpu
from jax.sharding import PartitionSpec as P

H = 12
HD = 64
FF = 1152
PAIR = 2 * HD

rope_base = 160000.0
norm_eps = 1e-05
f32 = jnp.float32
bf16 = jnp.bfloat16


def dot(a, b, dims):
    return lax.dot_general(a, b, (dims, ((), ())), preferred_element_type=f32)


NN = ((1,), (0,))
NT = ((1,), (1,))
TN = ((0,), (0,))


def attend_kernel(q_ref, k_ref, v_ref, o_ref, lse_ref):
    outs, totals = [], []
    for half in range(2):
        cols = slice(half * HD, (half + 1) * HD)
        scores = dot(q_ref[:, cols], k_ref[:, cols], NT) * 0.125
        largest = jnp.max(scores, axis=-1, keepdims=True)
        weights = jnp.exp(scores - largest)
        total = jnp.sum(weights, axis=-1, keepdims=True)
        outs.append(dot(weights.astype(bf16), v_ref[:, cols], NN) / total)
        totals.append(jnp.broadcast_to(largest + jnp.log(total), outs[-1].shape))
    o_ref[...] = jnp.concatenate(outs, axis=-1).astype(bf16)
    lse_ref[...] = jnp.concatenate(totals, axis=-1)


def attend_back_kernel(q_ref, k_ref, v_ref, do_ref, lse_ref, dq_ref, dk_ref, dv_ref):
    dqs, dks, dvs = [], [], []
    for half in range(2):
        cols = slice(half * HD, (half + 1) * HD)
        q, k, v, do = q_ref[:, cols], k_ref[:, cols], v_ref[:, cols], do_ref[:, cols]
        scores = dot(q, k, NT) * 0.125
        probabilities = jnp.exp(scores - lse_ref[:, half * HD : half * HD + 1])
        grad_probs = dot(do, v, NT)
        delta = jnp.sum(probabilities * grad_probs, axis=-1, keepdims=True)
        grad_scores = (probabilities * (grad_probs - delta)).astype(bf16)
        dqs.append(dot(grad_scores, k, NN) * 0.125)
        dks.append(dot(grad_scores, q, TN) * 0.125)
        dvs.append(dot(probabilities.astype(bf16), do, TN))
    dq_ref[...] = jnp.concatenate(dqs, axis=-1)
    dk_ref[...] = jnp.concatenate(dks, axis=-1).astype(bf16)
    dv_ref[...] = jnp.concatenate(dvs, axis=-1).astype(bf16)


def column_blocks(rows):
    return pl.BlockSpec((rows, PAIR), lambda h: (0, h))


def attend(q, k, v):
    rows, width = q.shape
    keys = k.shape[0]
    return pl.pallas_call(
        attend_kernel,
        grid=(width // PAIR,),
        in_specs=[column_blocks(rows), column_blocks(keys), column_blocks(keys)],
        out_specs=[column_blocks(rows), column_blocks(rows)],
        out_shape=[
            jax.ShapeDtypeStruct((rows, width), bf16),
            jax.ShapeDtypeStruct((rows, width), f32),
        ],
        compiler_params=pltpu.CompilerParams(vmem_limit_bytes=50 * 2**20),
        cost_estimate=pl.CostEstimate(
            flops=4 * rows * keys * width,
            bytes_accessed=8 * (rows + keys) * width,
            transcendentals=rows * keys * H,
        ),
    )(q, k, v)


def attend_back(q, k, v, do, lse):
    rows, width = q.shape
    keys = k.shape[0]
    return pl.pallas_call(
        attend_back_kernel,
        grid=(width // PAIR,),
        in_specs=[
            column_blocks(rows),
            column_blocks(keys),
            column_blocks(keys),
            column_blocks(rows),
            column_blocks(rows),
        ],
        out_specs=[column_blocks(rows), column_blocks(keys), column_blocks(keys)],
        out_shape=[
            jax.ShapeDtypeStruct((rows, width), f32),
            jax.ShapeDtypeStruct((keys, width), bf16),
            jax.ShapeDtypeStruct((keys, width), bf16),
        ],
        compiler_params=pltpu.CompilerParams(vmem_limit_bytes=50 * 2**20),
        cost_estimate=pl.CostEstimate(
            flops=10 * rows * keys * width,
            bytes_accessed=12 * (rows + keys) * width,
            transcendentals=rows * keys * H,
        ),
    )(q, k, v, do, lse)


def turn(values):
    column = lax.broadcasted_iota(jnp.int32, values.shape, 1)
    ahead = jnp.concatenate([values[:, HD // 2 :], values[:, : HD // 2]], axis=1)
    behind = jnp.concatenate([values[:, -(HD // 2) :], values[:, : -(HD // 2)]], axis=1)
    return jnp.where(column % HD < HD // 2, -ahead, behind)


def rotate(values, cosines, sines):
    return values * cosines + turn(values) * sines


def unrotate(values, cosines, sines):
    return values * cosines - turn(values * sines)


def normalize(values):
    average = jnp.mean(values, axis=-1, keepdims=True)
    centred = values - average
    variance = jnp.mean(centred * centred, axis=-1, keepdims=True)
    scale = lax.rsqrt(variance + norm_eps)
    return centred * scale, scale


def norm_back(e, xhat, scale):
    return scale * (
        e - jnp.mean(e, axis=-1, keepdims=True) - xhat * jnp.mean(e * xhat, axis=-1, keepdims=True)
    )


def body(seqs_here, group, tokens, w_qkv, w_attn, w_in, w_mlp, gain_one, gain_two, cotangent):
    block_rows, width = tokens.shape[1:]
    ctx = seqs_here * group
    me = lax.axis_index("ctx")
    mine, place = me // group, me % group

    def hop(block, distance):
        route = [(i, (i + distance * group) % ctx) for i in range(ctx)]
        return lax.ppermute(block, "ctx", route)

    def to_sequence(values):
        parts = [lax.dynamic_index_in_dim(values, mine, 0, keepdims=False)]
        for d in range(1, seqs_here):
            part = lax.dynamic_index_in_dim(values, (mine + d) % seqs_here, 0, keepdims=False)
            parts.append(hop(part, d))
        return jnp.concatenate(parts, axis=0)

    def from_sequence(values):
        parts = [values[:block_rows]]
        for d in range(1, seqs_here):
            parts.append(hop(values[d * block_rows : (d + 1) * block_rows], -d))
        stacked = jnp.stack(parts + parts)
        return lax.dynamic_slice_in_dim(stacked, (seqs_here - mine) % seqs_here, seqs_here, 0)

    groups = [[q * group + r for r in range(group)] for q in range(seqs_here)]
    swap = [(i, i ^ 1) for i in range(ctx)]

    def share_keys(k, v):
        if group == 2:
            other = lax.ppermute(jnp.stack([k, v]), "ctx", swap)
            return jnp.concatenate([k, other[0]]), jnp.concatenate([v, other[1]])
        both = lax.all_gather(jnp.stack([k, v]), "ctx", axis=1, tiled=True, axis_index_groups=groups)
        return both[0], both[1]

    def sum_keys(dk, dv):
        rows = dk.shape[0] // group
        if group == 2:
            other = lax.ppermute(jnp.stack([dk[rows:], dv[rows:]]), "ctx", swap)
            return (
                dk[:rows].astype(f32) + other[0].astype(f32),
                dv[:rows].astype(f32) + other[1].astype(f32),
            )
        both = lax.psum_scatter(
            jnp.stack([dk, dv]), "ctx", scatter_dimension=1, axis_index_groups=groups, tiled=True
        ).astype(f32)
        return both[0], both[1]

    core = me % 2
    parity = [[i for i in range(ctx) if i % 2 == r] for r in range(2)]

    def half_of(values, which):
        half = values.shape[1] // 2
        return lax.dynamic_slice_in_dim(values, which * half, half, 1)

    def join(own, other):
        left = jnp.where(core == 0, own, other)
        right = jnp.where(core == 0, other, own)
        return jnp.concatenate([left, right], axis=1)

    def gather(shard):
        return lax.all_gather(half_of(shard, core), "seq", axis=0, tiled=True)

    def both_halves(own):
        return join(own, lax.ppermute(own, "ctx", swap))

    def reduce_pair(left, right):
        sent = dot(left, half_of(right, 1 - core), TN).astype(bf16)
        got = lax.ppermute(sent, "ctx", swap)
        kept = dot(left, half_of(right, core), TN) + got.astype(f32)
        return kept.astype(bf16)

    def scatter(kept):
        return lax.psum_scatter(kept, "seq", scatter_dimension=0, tiled=True)

    mlp_rows, attn_rows = w_mlp.shape[0], w_attn.shape[0]
    narrow = width // 2

    def pack(mlp, attn, wide):
        wide = wide.reshape(-1, attn_rows, wide.shape[1])
        blocks = [wide[:, :, i : i + narrow] for i in range(0, wide.shape[2], narrow)]
        rows = [mlp.reshape(-1, mlp_rows, narrow), attn.reshape(-1, attn_rows, narrow)]
        return jnp.concatenate(rows + blocks, axis=1)

    def unpack(packed):
        start = mlp_rows + attn_rows
        ends = range(start, packed.shape[1], attn_rows)
        blocks = [packed[:, i : i + attn_rows].reshape(-1, narrow) for i in ends]
        return (
            packed[:, :mlp_rows].reshape(-1, narrow),
            packed[:, mlp_rows:start].reshape(-1, narrow),
            jnp.concatenate(blocks, axis=1),
        )

    def join_packed(own):
        other = lax.ppermute(own, "ctx", swap)
        return [join(a, b) for a, b in zip(unpack(own), unpack(other))]

    gain_one = gain_one.astype(f32)[:, None]
    gain_two = gain_two.astype(f32)[:, None]
    qkv_all = both_halves(gather((w_qkv.astype(f32) * gain_one).astype(bf16)))
    scaled_in = (w_in.astype(f32) * gain_two).astype(bf16)
    packed = pack(half_of(w_mlp, core), half_of(w_attn, core), half_of(scaled_in, core))
    packed = lax.all_gather(packed, "seq", axis=0, tiled=True)

    x = to_sequence(tokens).astype(f32)
    g = to_sequence(cotangent)

    came_from = (mine - jnp.arange(seqs_here, dtype=jnp.int32)) % seqs_here
    starts = (came_from * group + place) * block_rows
    positions = (starts[:, None] + jnp.arange(block_rows, dtype=jnp.int32)).reshape(-1)
    frequency = rope_base ** (-(jnp.arange(HD // 2, dtype=f32) * 2.0) / HD)
    angles = positions.astype(f32)[:, None] * frequency[None, :]
    cosines = jnp.tile(jnp.cos(angles), (1, 2 * H))
    sines = jnp.tile(jnp.sin(angles), (1, 2 * H))

    xhat, scale_one = normalize(x)
    h1 = xhat.astype(bf16)
    qkv = dot(h1, qkv_all, NN)
    q = rotate(qkv[:, :width], cosines, sines).astype(bf16)
    k = rotate(qkv[:, width : 2 * width], cosines, sines).astype(bf16)
    v = qkv[:, 2 * width :].astype(bf16)
    keys, values = share_keys(k, v)
    attn, lse = attend(q, keys, values)
    attn, packed = lax.optimization_barrier((attn, packed))
    mlp_all, attn_all, in_all = join_packed(packed)
    x2 = x + dot(attn, attn_all, NN)
    xhat2, scale_two = normalize(x2)
    h2 = xhat2.astype(bf16)
    gu = dot(h2, in_all, NN)
    gate, up = gu[:, :FF], gu[:, FF:]
    cumulative = 0.5 * (1.0 + lax.erf(gate * (0.5**0.5)))
    gelu = gate * cumulative
    slope = cumulative + gate * jnp.exp(-0.5 * gate * gate) * 0.3989422804014327
    a = (gelu * up).astype(bf16)
    layer_output = from_sequence((x2 + dot(a, mlp_all, NN)).astype(bf16))
    part_mlp = reduce_pair(a, g)
    da = dot(g, mlp_all, NT)
    dgu = jnp.concatenate([da * up * slope, da * gelu], axis=-1).astype(bf16)
    part_in = reduce_pair(h2, dgu)
    dx2 = g.astype(f32) + norm_back(dot(dgu, in_all, NT), xhat2, scale_two)
    dy = dx2.astype(bf16)
    part_attn = reduce_pair(attn, dy)
    do = dot(dy, attn_all, NT).astype(bf16)
    part = pack(part_mlp, part_attn, part_in)
    do, part = lax.optimization_barrier((do, part))
    part = scatter(part)
    dq, dk, dv = attend_back(q, keys, values, do, lse)
    dk, dv = sum_keys(dk, dv)
    dqkv = jnp.concatenate(
        [unrotate(dq, cosines, sines), unrotate(dk, cosines, sines), dv], axis=-1
    ).astype(bf16)
    part_qkv = scatter(reduce_pair(h1, dqkv))
    blocks = [part_qkv[None, :, i : i + narrow] for i in range(0, part_qkv.shape[1], narrow)]
    part = lax.psum(jnp.concatenate([part] + blocks, axis=1), "ctx", axis_index_groups=parity)
    other = lax.ppermute(part, "ctx", swap)
    (mlp_own, attn_own, wide_own), (mlp_got, attn_got, wide_got) = unpack(part), unpack(other)
    grad_mlp = join(mlp_own, mlp_got).astype(f32)
    grad_attn = join(attn_own, attn_got).astype(f32)
    middle = w_in.shape[1] // 2
    raw_in = join(wide_own[:, :middle], wide_got[:, :middle]).astype(f32)
    raw_qkv = join(wide_own[:, middle:], wide_got[:, middle:]).astype(f32)
    dx = dx2 + norm_back(dot(dqkv, qkv_all, NT), xhat, scale_one)
    grad_tokens = from_sequence(dx.astype(bf16)).astype(f32)
    return (
        layer_output,
        grad_tokens,
        raw_qkv * gain_one,
        grad_attn,
        raw_in * gain_two,
        grad_mlp,
        jnp.sum(raw_qkv * w_qkv.astype(f32), axis=-1),
        jnp.sum(raw_in * w_in.astype(f32), axis=-1),
    )


def solution(mesh):
    split = P("seq", "ctx", None)
    rows = P("seq", None)

    def whole(tokens, *others):
        seqs_here = tokens.shape[0] // mesh.shape["seq"]
        group = mesh.shape["ctx"] // seqs_here
        return jax.shard_map(
            functools.partial(body, seqs_here, group),
            mesh=mesh,
            in_specs=(split, rows, rows, rows, rows, P("seq"), P("seq"), split),
            out_specs=(split, split, rows, rows, rows, rows, P("seq"), P("seq")),
            check_vma=False,
        )(tokens, *others)

    return whole
```
